32 devices in a mesh: spec: 4 (over x, core), space: 8 (over z, y).
Axes of the slice: x: 2, y: 2, z: 4, core: 2. Of those that a mesh axis runs over, the one named last changes fastest.
Arguments:
- spectra: float32 [768, 32, 128], P(None, ('space', 'spec')), may hold values from -6 to 6
- quad_first: bfloat16 [768, 768], replicated, may hold values from -0.21875 to 0.21875
- quad_second: bfloat16 [768, 768], replicated, may hold values from -0.21875 to 0.21875
- quad_output: bfloat16 [768, 768], replicated, may hold values from -0.21875 to 0.21875
- owner_map: int32 [8], replicated, may hold values from 0 to 2
- land_mask: int32 [32, 128], P('space'), may hold values 0 or 1
- nest_dest: int32 [512], P('space'), may hold values from 0 to 7, as said below
- nest_src: int32 [512], P('space'), may hold values from 0 to 511
- nest_into: int32 [512], P('space'), may hold values from 0 to 511
Outputs:
- spectra_out: float32 [768, 32, 128], P(None, ('space', 'spec'))
The draws below stay inside these ranges and needn't reach their ends.
Inputs may be any that keep to these rules, and one draw needn't show every extreme that they name: `nest_dest`: among the 64 entries of each tile no tile is named more than 16 times, and one tile is named exactly 16 times by the entries of every tile.
All inputs are finite; a program needn't handle non-finite values. No bound on the sum of `land_mask` on one device may be relied on, other than what follows from the above.
Results may differ from the reference program's by a relative error of at most 0.0016.
Values sent between devices are 32-bit elements; how exact they have to be, the bound alone decides.
A program may use at most 64 MiB of HBM per device.

```python
import math
import jax
import jax.numpy as jnp
from jax import lax

BINS = 768
DIRS = 24
LON = 128
SUBSTEPS = 6
GRIDS = 3
CAP = 16
FREQS = 32
TILES = 8
LAT = 32
SEND_DEV = 64
N_SPEC = 4


def draw_nest_dest(key, part):
    busiest = jax.random.randint(jax.random.fold_in(key, 7), (), 0, TILES).astype(jnp.int32)
    repeated = (jnp.arange((TILES - 1) * CAP, dtype=jnp.int32) // CAP).astype(jnp.int32)
    others = repeated + (repeated >= busiest).astype(jnp.int32)

    def sender(sender_index):
        first_key = jax.random.fold_in(jax.random.fold_in(key, 11), sender_index)
        second_key = jax.random.fold_in(jax.random.fold_in(key, 13), sender_index)
        picked = jax.random.permutation(first_key, others)[:SEND_DEV - CAP]
        entries = jnp.concatenate([jnp.full((CAP,), busiest, dtype=jnp.int32), picked.astype(jnp.int32)])
        return jax.random.permutation(second_key, entries)
    return jax.vmap(sender)(jnp.arange(TILES, dtype=jnp.int32)).reshape(TILES * SEND_DEV).astype(jnp.int32)


def set_ends(values, rng, least, high):
    dims = values.shape
    place = [jax.random.randint(jax.random.fold_in(rng, axis), (), 0, dims[axis]) for axis in range(len(dims))]
    values = values.at[tuple(place)].set(least)
    longest = dims.index(max(dims))
    place[longest] = (place[longest] + 1) % dims[longest]
    return values.at[tuple(place)].set(high)


def shard_levels(own_key, shape, pieces, smallest, high):
    gain, own = 1.0, jax.random.fold_in(own_key, 6)
    for position, blocks in pieces:
        steps = jnp.exp(jax.random.uniform(jax.random.fold_in(own, position), (blocks,), jnp.float32, smallest / len(pieces), high / len(pieces)))
        gain = gain * jnp.repeat(steps, shape[position] // blocks).reshape([-1 if axis == position else 1 for axis in range(len(shape))])
    return gain


def noise(own_key, extent, width, limit, split=(), held_as=jnp.bfloat16):
    loudness = shard_levels(own_key, extent, split, -0.22, 0.18) if split else 1.0
    result = jax.random.normal(own_key, extent, jnp.float32) * width * loudness
    return jnp.minimum(jnp.maximum(result, -limit), limit).astype(held_as)


def setup_inputs(seed: int = 0) -> dict:
    seeds = jax.random.split(jax.random.key(seed), 10)
    return {
        "spectra": noise(seeds[0], (BINS, LAT, LON), 1.0, 6.0, ((1, 32),), jnp.float32),
        "quad_first": noise(seeds[1], (BINS, BINS), BINS ** -0.5, 0.21875),
        "quad_second": noise(seeds[2], (BINS, BINS), BINS ** -0.5, 0.21875),
        "quad_output": noise(seeds[3], (BINS, BINS), BINS ** -0.5, 0.21875),
        "owner_map": set_ends(jax.random.randint(seeds[4], (TILES,), 0, GRIDS), jax.random.fold_in(seeds[4], 1), 0, GRIDS - 1).astype(jnp.int32),
        "land_mask": set_ends((jax.random.randint(seeds[5], (LAT, LON), 0, 10) < 7).astype(jnp.int32), jax.random.fold_in(seeds[5], 1), 0, 1),
        "nest_dest": draw_nest_dest(jax.random.fold_in(seeds[9], 71), 0),
        "nest_src": set_ends(jax.random.randint(seeds[7], (TILES * SEND_DEV,), 0, N_SPEC * LON), jax.random.fold_in(seeds[7], 1), 0, (N_SPEC * LON) - 1).astype(jnp.int32),
        "nest_into": set_ends(jax.random.randint(seeds[8], (TILES * SEND_DEV,), 0, N_SPEC * LON), jax.random.fold_in(seeds[8], 1), 0, (N_SPEC * LON) - 1).astype(jnp.int32),
    }


step_weight = 0.25
grid_factors = (1.0, 0.55, 0.3)


def minmod(lower_diff, upper_diff):
    return 0.5 * (jnp.sign(lower_diff) + jnp.sign(upper_diff)) * jnp.minimum(jnp.abs(lower_diff), jnp.abs(upper_diff))


def upwind_sweep(padded, courant, forward, axis_index):
    length = padded.shape[axis_index]
    differences = lax.slice_in_dim(padded, 1, length, axis=axis_index) - lax.slice_in_dim(padded, 0, length - 1, axis=axis_index)
    slopes = minmod(lax.slice_in_dim(differences, 0, length - 2, axis=axis_index), lax.slice_in_dim(differences, 1, length - 1, axis=axis_index))
    centres = lax.slice_in_dim(padded, 1, length - 1, axis=axis_index)
    upper_flux = courant * (centres + 0.5 * (1.0 - courant) * slopes)
    lower_flux = courant * (centres - 0.5 * (1.0 + courant) * slopes)
    face_count = length - 3
    fluxes = jnp.where(forward, lax.slice_in_dim(upper_flux, 0, face_count, axis=axis_index), lax.slice_in_dim(lower_flux, 1, face_count + 1, axis=axis_index))
    interior = lax.slice_in_dim(padded, 2, length - 2, axis=axis_index)
    return interior - (lax.slice_in_dim(fluxes, 1, face_count, axis=axis_index) - lax.slice_in_dim(fluxes, 0, face_count - 1, axis=axis_index))


def bin_speeds(first_bin, bin_count):
    indices = first_bin + jnp.arange(bin_count, dtype=jnp.int32)
    freq_index = (indices // DIRS).astype(jnp.float32)
    direction = ((indices % DIRS).astype(jnp.float32) + 0.5) * (2.0 * math.pi / DIRS)
    speeds = 0.2 + 0.7 * (freq_index + 0.5) / FREQS
    return speeds * jnp.cos(direction), speeds * jnp.sin(direction)


def row_scales(owner_map, first_row, row_count, tile_rows):
    rows_here = first_row + jnp.arange(row_count, dtype=jnp.int32)
    tile_of = jnp.clip(rows_here // tile_rows, 0, owner_map.shape[0] - 1)
    matches = tile_of[:, None] == jnp.arange(owner_map.shape[0], dtype=jnp.int32)[None, :]
    grid_of = jnp.sum(jnp.where(matches, owner_map[None, :], 0), axis=1)
    scales = jnp.where(grid_of == 0, grid_factors[0], jnp.where(grid_of == 1, grid_factors[1], grid_factors[2]))
    return scales.astype(jnp.float32)


def substep(padded, scales, sea_rows, north_speed, east_speed):
    lat_courant = north_speed[:, None, None] * scales[None, 1:-1, None]
    advected = upwind_sweep(padded, lat_courant, (north_speed > 0)[:, None, None], 1)
    lon_padded = jnp.concatenate([advected[:, :, -2:], advected, advected[:, :, :2]], axis=2)
    lon_courant = east_speed[:, None, None] * scales[None, 2:-2, None]
    advected = upwind_sweep(lon_padded, lon_courant, (east_speed > 0)[:, None, None], 2)
    return advected * sea_rows[None]


def source_update(state_field, quad_first, quad_second, quad_output):
    contract = (((0,), (0,)), ((), ()))
    outline = state_field.shape
    matrix = state_field.reshape(outline[0], -1)
    rounded = matrix.astype(jnp.bfloat16)
    linear_one = lax.dot_general(quad_first, rounded, contract, preferred_element_type=jnp.float32)
    linear_two = lax.dot_general(quad_second, rounded, contract, preferred_element_type=jnp.float32)
    product = (linear_one * linear_two).astype(jnp.bfloat16)
    tendency = lax.dot_general(quad_output, product, contract, preferred_element_type=jnp.float32)
    return (matrix + step_weight * tendency).reshape(outline)


def reference(spectra, quad_first, quad_second, quad_output, owner_map, land_mask, nest_dest, nest_src, nest_into):
    sea_mask = land_mask.astype(jnp.float32)
    lat_rows = spectra.shape[1]
    lon_cols = spectra.shape[2]
    state_field = source_update(spectra, quad_first, quad_second, quad_output) * sea_mask[None]
    north_speed, east_speed = bin_speeds(0, BINS)
    scales = row_scales(owner_map, -2, lat_rows + 4, N_SPEC)

    def propagate(blocks):
        block_field, block_north, block_east = blocks
        for counter in range(SUBSTEPS):
            padded = jnp.pad(block_field, ((0, 0), (2, 2), (0, 0)))
            block_field = substep(padded, scales, sea_mask, block_north, block_east)
        return block_field

    grouped = lax.map(propagate, (state_field.reshape(FREQS, DIRS, lat_rows, lon_cols), north_speed.reshape(FREQS, DIRS), east_speed.reshape(FREQS, DIRS)))
    flat_field = grouped.reshape(BINS, lat_rows * lon_cols)
    tile_points = N_SPEC * lon_cols
    senders = jnp.arange(TILES * SEND_DEV, dtype=jnp.int32) // SEND_DEV
    source_cells = senders * tile_points + nest_src
    target_cells = nest_dest * tile_points + nest_into
    totals = jnp.zeros_like(flat_field).at[:, target_cells].add(flat_field[:, source_cells])
    counts = jnp.zeros((lat_rows * lon_cols,), jnp.float32).at[target_cells].add(jnp.ones((TILES * SEND_DEV,), jnp.float32))
    merged = (flat_field + totals) / (1.0 + counts)[None, :]
    finished = source_update(merged.reshape(BINS, lat_rows, lon_cols), quad_first, quad_second, quad_output)
    return finished * sea_mask[None]
```

```python
import functools
import math

import jax
import jax.numpy as jnp
from jax import lax
from jax.experimental import pallas as pl
from jax.experimental.pallas import tpu as pltpu
from jax.sharding import PartitionSpec as P

DIRS = 24
SUBSTEPS = 6
FREQS = 32
PARTS = 1

step_weight = 0.25
grid_factors = (1.0, 0.55, 0.3)

F32 = jnp.float32
BF16 = jnp.bfloat16
MESH = pl.DeviceIdType.MESH


def minmod(a, b):
    return jnp.maximum(jnp.minimum(a, 0.0), jnp.minimum(b, jnp.maximum(a, 0.0)))


def split_high_low(x):
    high = x.astype(BF16)
    return high, (x - high.astype(F32)).astype(BF16)


def repeat(count, body):
    if count <= 4:
        for i in range(count):
            body(i)
    else:
        lax.fori_loop(0, count, lambda i, c: (body(i), c)[1], 0)


def kernel(
    dims,
    spectra, quad_first, quad_second, quad_output, owner, land, dest, src, into,
    out,
    field, w1, w2, w3, outbox, cells, inbox, meta, ent, mask_b, inv_b, coef, speed, oh_src, oh_dst, gathered,
    load_sem, meta_send, meta_recv, go_send, go_recv, back_send, back_recv,
):
    n, tiles, spec, bins, lon, band, parts, pband, entries = dims
    rows = n
    shift = lon.bit_length() - 1
    spec_rank = lax.axis_index("spec")
    tile = lax.axis_index("space")
    me = tile * spec + spec_rank

    loads = [
        pltpu.make_async_copy(a, b, load_sem.at[i])
        for i, (a, b) in enumerate(
            ((spectra, field), (quad_first, w1), (quad_second, w2), (quad_output, w3))
        )
    ]
    for copy in loads:
        copy.start()

    def target(q):
        return {"space": lax.div(q, spec), "spec": lax.rem(q, spec)}

    def peer(k):
        half = lax.div(k + 1, 2)
        offset = n // 2 + half * (1 - 2 * lax.rem(k, 2))
        return lax.rem(me + offset, n)

    barrier = pltpu.get_barrier_semaphore()

    def greet(k, c):
        pl.semaphore_signal(barrier, inc=1, device_id=target(peer(k)), device_id_type=MESH)
        return c

    lax.fori_loop(0, n - 1, greet, 0)

    width = min(entries, lon)
    per = lon // width
    erows = entries // width
    base = -(-spec // 8) * 8
    mine = jnp.zeros(meta.shape[1:], jnp.int32)
    meta[tile] = mine
    meta[tile, 0:spec, :] = land[...]
    for j, part in enumerate((dest, src, into)):
        meta[tile, base + j * erows : base + (j + 1) * erows, 0:width] = part[...]
    own_mask = land[pl.ds(spec_rank, 1), :].astype(F32)

    pl.semaphore_wait(barrier, n - 1)

    def meta_copy(k):
        return pltpu.make_async_remote_copy(
            src_ref=meta.at[tile],
            dst_ref=meta.at[tile],
            send_sem=meta_send,
            recv_sem=meta_recv,
            device_id={"space": lax.rem(tile + k, tiles), "spec": spec_rank},
            device_id_type=MESH,
        )

    def send_meta(k, c):
        meta_copy(k).start()
        return c

    lax.fori_loop(1, tiles, send_meta, 0)

    def source(x):
        xt = x.T.astype(BF16)
        one = jnp.dot(xt, w1[...], preferred_element_type=F32)
        two = jnp.dot(xt, w2[...], preferred_element_type=F32)
        product = (one * two).astype(BF16)
        tendency = jnp.dot(product, w3[...], preferred_element_type=F32)
        return x + step_weight * tendency.T

    for copy in loads:
        copy.wait()
    sourced = source(field[...]) * own_mask
    if band % 8 == 0:
        outbox[...] = sourced.reshape(n, parts, pband, lon)
    else:
        field[...] = sourced
        outbox[...] = jnp.zeros_like(outbox)
        for q in range(n):
            outbox[q, 0, 0:band, :] = field[q * band : (q + 1) * band, :]

    for p in range(parts):

        def send(k, c):
            q = peer(k)
            pltpu.make_async_remote_copy(
                src_ref=outbox.at[q, p],
                dst_ref=cells.at[p, me],
                send_sem=go_send.at[p],
                recv_sem=go_recv.at[p],
                device_id=target(q),
                device_id_type=MESH,
            ).start()
            return c

        lax.fori_loop(0, n - 1, send, 0)
        cells[p, me] = outbox[me, p]

    local = lax.broadcasted_iota(jnp.int32, (parts * pband, lon), 0)
    index = (local + me * band).astype(F32)
    freq = jnp.floor((index + 0.5) * (1.0 / DIRS))
    direction = (index - DIRS * freq + 0.5) * (2.0 * math.pi / DIRS)
    speeds = 0.2 + 0.7 * (freq + 0.5) / FREQS
    speed[0] = speeds * jnp.cos(direction)
    speed[1] = speeds * jnp.sin(direction)
    for t in range(tiles):
        grid = owner[t]
        factor = jnp.where(
            grid == 0, grid_factors[0], jnp.where(grid == 1, grid_factors[1], grid_factors[2])
        ).astype(F32)
        for axis in range(2):
            courant = speed[axis] * factor
            coef[2 * axis, t] = jnp.abs(courant)
            coef[2 * axis + 1, t] = 0.5 * courant * (1.0 - jnp.abs(courant))

    drained = pltpu.make_async_copy(
        meta.at[pl.ds(0, tiles - 1)], meta.at[pl.ds(0, tiles - 1)], meta_recv
    )
    drained.wait()
    lanes = lax.broadcasted_iota(jnp.int32, (1, lon), 1)
    for t in range(tiles):
        sea = meta[t, 0:spec, :].astype(F32)
        for r in range(spec):
            mask_b[t * spec + r] = jnp.broadcast_to(sea[r : r + 1, :], mask_b.shape[1:])
    for u in range(tiles * erows // per):
        packed = [jnp.zeros((1, lon), jnp.int32) for _ in range(4)]
        for v in range(per):
            t = (u * per + v) // erows
            line = (u * per + v) % erows
            d, s, i = (
                meta[t, base + j * erows + line : base + j * erows + line + 1, :] for j in range(3)
            )
            values = (
                t * spec + lax.shift_right_logical(s, shift),
                s & (lon - 1),
                d * spec + lax.shift_right_logical(i, shift),
                i & (lon - 1),
            )
            here = (lanes >= v * width) & (lanes < (v + 1) * width)
            for j in range(4):
                moved = pltpu.roll(values[j], v * width, 1) if v else values[j]
                packed[j] = jnp.where(here, moved, packed[j])
        for j in range(4):
            ent[j, u] = jnp.broadcast_to(packed[j], ent.shape[2:])

    chunk = oh_src.shape[2]
    lines = chunk // lon
    chunks = tiles * entries // chunk
    chunk_tiles = chunk // entries
    crows = chunk_tiles * spec

    def wide(j, c):
        return jnp.concatenate([ent[j, c * lines + v] for v in range(lines)], axis=1)

    def hots(c):
        column = lax.broadcasted_iota(jnp.int32, (lon, chunk), 0)
        one = jnp.where(column == wide(1, c)[0:1, :], 1.0, 0.0).astype(BF16)
        oh_src[c, 0:lon, :] = one
        oh_src[c, lon : 2 * lon, :] = one
        two = jnp.where(column == wide(3, c)[0:1, :], 1.0, 0.0).astype(BF16)
        oh_dst[c, :, 0:chunk] = two
        oh_dst[c, :, chunk : 2 * chunk] = two

    repeat(chunks, hots)
    contract_last = (((1,), (1,)), ((), ()))
    row_block = min(rows, 32)
    for first in range(0, rows, row_block):

        def count(c, total):
            row = lax.broadcasted_iota(jnp.int32, (row_block, chunk), 0) + first
            one = jnp.where(row == wide(2, c)[0:1, :], 1.0, 0.0).astype(BF16)
            return total + lax.dot_general(
                one, oh_dst[c, :, 0:chunk], contract_last, preferred_element_type=F32
            )

        total = lax.fori_loop(0, chunks, count, jnp.zeros((row_block, lon), F32))
        share = 1.0 / (1.0 + total)
        for r in range(row_block):
            inv_b[first + r] = jnp.broadcast_to(share[r : r + 1, :], inv_b.shape[1:])

    def transport(p):
        def substep(step, carry):
            for b in range(pband // 8):
                sub = slice(b * 8, (b + 1) * 8)
                at = slice(p * pband + b * 8, p * pband + (b + 1) * 8)
                north = speed[0, at, :] > 0
                east = speed[1, at, :] > 0
                zero = jnp.zeros((8, lon), F32)
                prior_flux, prior_diff = zero, None
                current = cells[p, 0, sub, :]
                ahead = cells[p, 1, sub, :]
                prior_diff = current
                flux, held = None, None

                def finish(i, value, below, flux, above):
                    t = i // spec
                    value = value - flux + jnp.where(north, below, above)
                    diff = pltpu.roll(value, lon - 1, 1) - value
                    slope = minmod(pltpu.roll(diff, 1, 1), diff)
                    g = coef[2, t, at, :] * value + coef[3, t, at, :] * slope
                    upwind = jnp.where(east, pltpu.roll(g, 1, 1), pltpu.roll(g, lon - 1, 1))
                    cells[p, i, sub, :] = (value - g + upwind) * mask_b[i]

                before, flux, held = zero, None, None
                for i in range(rows):
                    t = i // spec
                    diff = ahead - current
                    slope = minmod(prior_diff, diff)
                    g = coef[0, t, at, :] * current + coef[1, t, at, :] * slope
                    if i > 0:
                        finish(i - 1, held, before, flux, g)
                        before = flux
                    flux, held, prior_diff = g, current, diff
                    current = ahead
                    ahead = cells[p, i + 2, sub, :] if i + 2 < rows else zero
                finish(rows - 1, held, before, flux, zero)
            return carry

        lax.fori_loop(0, SUBSTEPS, substep, 0)

    def nest(p):
        def gather(c):
            x = cells[p, pl.ds(c * crows, crows)].reshape(crows * pband, lon)
            both = jnp.concatenate(split_high_low(x), axis=1)
            picked = jnp.dot(both, oh_src[c], preferred_element_type=F32)
            picked = picked.reshape(crows, pband, chunk)
            home = wide(0, c)[0:1, :] - c * crows
            total = jnp.where(home == 0, picked[0], 0.0)
            for r in range(1, crows):
                total = total + jnp.where(home == r, picked[r], 0.0)
            gathered[c] = total

        repeat(chunks, gather)
        for first in range(0, rows, row_block):

            def scatter(c, total):
                high, low = split_high_low(gathered[c])
                both = jnp.concatenate([high.astype(F32), low.astype(F32)], axis=1)
                home = wide(2, c)[0:1, :]
                home = jnp.concatenate([home, home], axis=1)
                left = [
                    jnp.where(home == first + r, both, 0.0) for r in range(row_block)
                ]
                left = jnp.concatenate(left, axis=0).astype(BF16)
                return total + lax.dot_general(
                    left, oh_dst[c], contract_last, preferred_element_type=F32
                )

            total = jnp.zeros((row_block * pband, lon), F32)
            if chunks <= 4:
                for c in range(chunks):
                    total = scatter(c, total)
            else:
                total = lax.fori_loop(0, chunks, scatter, total)
            total = total.reshape(row_block, pband, lon)
            for r in range(row_block):
                for b in range(pband // 8):
                    sub = slice(b * 8, (b + 1) * 8)
                    cells[p, first + r, sub, :] = (
                        cells[p, first + r, sub, :] + total[r, sub, :]
                    ) * inv_b[first + r]

    for p in range(parts):
        pltpu.make_async_copy(
            cells.at[p, pl.ds(0, n - 1)], cells.at[p, pl.ds(0, n - 1)], go_recv.at[p]
        ).wait()
        transport(p)
        nest(p)

        def send_back(k, c):
            q = peer(k)
            pltpu.make_async_remote_copy(
                src_ref=cells.at[p, q],
                dst_ref=inbox.at[me, p],
                send_sem=back_send.at[p],
                recv_sem=back_recv,
                device_id=target(q),
                device_id_type=MESH,
            ).start()
            return c

        lax.fori_loop(0, n - 1, send_back, 0)
        inbox[me, p] = cells[p, me]

    pltpu.make_async_copy(
        inbox.at[pl.ds(0, n - 1)], inbox.at[pl.ds(0, n - 1)], back_recv
    ).wait()
    if band % 8 == 0:
        merged = inbox[...].reshape(bins, lon)
    else:
        for q in range(n):
            field[q * band : (q + 1) * band, :] = inbox[q, 0, 0:band, :]
        merged = field[...]
    out[...] = source(merged) * own_mask

    pltpu.make_async_copy(
        meta.at[pl.ds(0, tiles - 1)], meta.at[pl.ds(0, tiles - 1)], meta_send
    ).wait()
    for p in range(parts):
        sent = outbox.at[pl.ds(0, n - 1), p]
        pltpu.make_async_copy(sent, sent, go_send.at[p]).wait()
        sent = cells.at[p, pl.ds(0, n - 1)]
        pltpu.make_async_copy(sent, sent, back_send.at[p]).wait()


def shards(
    spectra,
    quad_first,
    quad_second,
    quad_output,
    owner_map,
    land_mask,
    nest_dest,
    nest_src,
    nest_into,
):
    spec = lax.axis_size("spec")
    tiles = lax.axis_size("space")
    n = spec * tiles
    bins, _, lon = spectra.shape
    band = bins // n
    parts = PARTS if band % (8 * PARTS) == 0 else 1
    pband = band // parts if band % 8 == 0 else -(-band // 8) * 8
    entries = nest_dest.shape[0]
    width = min(entries, lon)
    erows = entries // width
    meta_rows = -(-(-(-spec // 8) * 8 + 3 * erows) // 8) * 8
    total = tiles * entries
    chunk = max(entries, min(2 * lon, total))
    chunks = total // chunk
    dims = (n, tiles, spec, bins, lon, band, parts, pband, entries)
    vmem = pl.BlockSpec(memory_space=pltpu.VMEM)
    hbm = pl.BlockSpec(memory_space=pl.ANY)
    V = pltpu.VMEM
    dma = pltpu.SemaphoreType.DMA
    result = pl.pallas_call(
        functools.partial(kernel, dims),
        out_shape=jax.ShapeDtypeStruct((bins, lon), F32),
        in_specs=[hbm] * 4 + [pl.BlockSpec(memory_space=pltpu.SMEM)] + [vmem] * 4,
        out_specs=vmem,
        scratch_shapes=[
            V((bins, lon), F32),
            V(quad_first.shape, BF16),
            V(quad_second.shape, BF16),
            V(quad_output.shape, BF16),
            V((n, parts, pband, lon), F32),
            V((parts, n, pband, lon), F32),
            V((n, parts, pband, lon), F32),
            V((tiles, meta_rows, lon), jnp.int32),
            V((4, total // lon, 8, lon), jnp.int32),
            V((n, 8, lon), F32),
            V((n, 8, lon), F32),
            V((4, tiles, parts * pband, lon), F32),
            V((2, parts * pband, lon), F32),
            V((chunks, 2 * lon, chunk), BF16),
            V((chunks, lon, 2 * chunk), BF16),
            V((chunks, pband, chunk), F32),
            dma((4,)),
            dma,
            dma,
            dma((parts,)),
            dma((parts,)),
            dma((parts,)),
            dma,
        ],
        compiler_params=pltpu.CompilerParams(
            collective_id=0, has_side_effects=True, vmem_limit_bytes=48 * 1024 * 1024
        ),
        cost_estimate=pl.CostEstimate(
            flops=12 * bins * bins * lon, bytes_accessed=6 * bins * bins + 8 * bins * lon, transcendentals=0
        ),
    )(
        spectra.reshape(bins, lon),
        quad_first,
        quad_second,
        quad_output,
        owner_map,
        land_mask,
        nest_dest.reshape(erows, width),
        nest_src.reshape(erows, width),
        nest_into.reshape(erows, width),
    )
    return result.reshape(spectra.shape)


def solution(mesh):
    return jax.shard_map(
        shards,
        mesh=mesh,
        in_specs=(
            P(None, ("space", "spec"), None),
            P(),
            P(),
            P(),
            P(),
            P("space", None),
            P("space"),
            P("space"),
            P("space"),
        ),
        out_specs=P(None, ("space", "spec"), None),
        check_vma=False,
    )
```

```python
import functools
import math

import jax
import jax.numpy as jnp
from jax import lax
from jax.experimental import pallas as pl
from jax.experimental.pallas import tpu as pltpu
from jax.sharding import PartitionSpec as P

DIRS = 24
SUBSTEPS = 6
FREQS = 32
PARTS = 3

step_weight = 0.25
grid_factors = (1.0, 0.55, 0.3)

F32 = jnp.float32
BF16 = jnp.bfloat16
MESH = pl.DeviceIdType.MESH


def minmod(a, b):
    return jnp.maximum(jnp.minimum(a, 0.0), jnp.minimum(b, jnp.maximum(a, 0.0)))


def split_high_low(x):
    high = x.astype(BF16)
    return high, (x - high.astype(F32)).astype(BF16)


def repeat(count, body):
    if count <= 4:
        for i in range(count):
            body(i)
    else:
        lax.fori_loop(0, count, lambda i, c: (body(i), c)[1], 0)


def kernel(
    dims,
    spectra, quad_first, quad_second, quad_output, owner_in, land_in, dest_in, src_in, into_in,
    out,
    owner, land, dest, src, into, field, w1, w2, w3, outbox, cells, inbox, meta, ent, mask_b, inv_b, coef, speed, oh_src, oh_dst, gathered,
    load_sem, meta_send, meta_recv, go_send, go_recv, back_send, back_recv,
):
    n, tiles, spec, bins, lon, band, parts, pband, entries = dims
    rows = n
    shift = lon.bit_length() - 1
    spec_rank = lax.axis_index("spec")
    tile = lax.axis_index("space")
    me = tile * spec + spec_rank

    loads = [
        pltpu.make_async_copy(a, b, load_sem.at[i])
        for i, (a, b) in enumerate(
            (
                (land_in, land), (dest_in, dest), (src_in, src), (into_in, into), (owner_in, owner),
                (spectra, field), (quad_first, w1), (quad_second, w2), (quad_output, w3),
            )
        )
    ]
    for copy in loads:
        copy.start()

    def peers(visit):
        def one_tile(j, c):
            offset = tiles // 2 + lax.div(j + 1, 2) * (1 - 2 * lax.rem(j, 2))
            t = tile + offset
            t = jnp.where(t >= tiles, t - tiles, t)
            for k in range(spec):
                r = spec_rank + k
                visit(t, jnp.where(r >= spec, r - spec, r))
            return c

        lax.fori_loop(0, tiles - 1, one_tile, 0)
        for k in range(1, spec):
            r = spec_rank + k
            visit(tile, jnp.where(r >= spec, r - spec, r))

    barrier = pltpu.get_barrier_semaphore()

    def greet(t, r):
        pl.semaphore_signal(
            barrier, inc=1, device_id={"space": t, "spec": r}, device_id_type=MESH
        )

    peers(greet)

    width = min(entries, lon)
    per = lon // width
    erows = entries // width
    base = -(-spec // 8) * 8
    for copy in loads[:5]:
        copy.wait()
    mine = jnp.zeros(meta.shape[1:], jnp.int32)
    meta[tile] = mine
    meta[tile, 0:spec, :] = land[...]
    for j, part in enumerate((dest, src, into)):
        meta[tile, base + j * erows : base + (j + 1) * erows, 0:width] = part[...]
    own_mask = land[pl.ds(spec_rank, 1), :].astype(F32)

    def meta_copy(k):
        return pltpu.make_async_remote_copy(
            src_ref=meta.at[tile],
            dst_ref=meta.at[tile],
            send_sem=meta_send,
            recv_sem=meta_recv,
            device_id={"space": lax.rem(tile + k, tiles), "spec": spec_rank},
            device_id_type=MESH,
        )

    def send_meta(k, c):
        meta_copy(k).start()
        return c

    def source(x):
        xt = x.T.astype(BF16)
        one = jnp.dot(xt, w1[...], preferred_element_type=F32)
        two = jnp.dot(xt, w2[...], preferred_element_type=F32)
        product = (one * two).astype(BF16)
        tendency = jnp.dot(product, w3[...], preferred_element_type=F32)
        return x + step_weight * tendency.T

    for copy in loads[5:]:
        copy.wait()
    sourced = source(field[...]) * own_mask
    if band % 8 == 0:
        outbox[...] = sourced.reshape(n, parts, pband, lon)
    else:
        field[...] = sourced
        outbox[...] = jnp.zeros_like(outbox)
        for q in range(n):
            outbox[q, 0, 0:band, :] = field[q * band : (q + 1) * band, :]

    pl.semaphore_wait(barrier, n - 1)
    lax.fori_loop(1, tiles, send_meta, 0)

    def send_part(p, c):
        def send(t, r):
            pltpu.make_async_remote_copy(
                src_ref=outbox.at[t * spec + r, p],
                dst_ref=cells.at[p, me],
                send_sem=go_send.at[p],
                recv_sem=go_recv.at[p],
                device_id={"space": t, "spec": r},
                device_id_type=MESH,
            ).start()

        peers(send)
        cells[p, me] = outbox[me, p]
        return c

    lax.fori_loop(0, parts, send_part, 0)

    local = lax.broadcasted_iota(jnp.int32, (parts, pband, lon), 1)
    local = local + lax.broadcasted_iota(jnp.int32, (parts, pband, lon), 0) * pband
    index = (local + me * band).astype(F32)
    freq = jnp.floor((index + 0.5) * (1.0 / DIRS))
    direction = (index - DIRS * freq + 0.5) * (2.0 * math.pi / DIRS)
    speeds = 0.2 + 0.7 * (freq + 0.5) / FREQS
    speed[0] = speeds * jnp.cos(direction)
    speed[1] = speeds * jnp.sin(direction)
    for t in range(tiles):
        grid = owner[t]
        factor = jnp.where(
            grid == 0, grid_factors[0], jnp.where(grid == 1, grid_factors[1], grid_factors[2])
        ).astype(F32)
        for axis in range(2):
            courant = speed[axis] * factor
            coef[2 * axis, t] = jnp.abs(courant)
            coef[2 * axis + 1, t] = 0.5 * courant * (1.0 - jnp.abs(courant))

    drained = pltpu.make_async_copy(
        meta.at[pl.ds(0, tiles - 1)], meta.at[pl.ds(0, tiles - 1)], meta_recv
    )
    drained.wait()
    lanes = lax.broadcasted_iota(jnp.int32, (1, lon), 1)
    for t in range(tiles):
        sea = meta[t, 0:spec, :].astype(F32)
        for r in range(spec):
            mask_b[t * spec + r] = jnp.broadcast_to(sea[r : r + 1, :], mask_b.shape[1:])
    for u in range(tiles * erows // per):
        packed = [jnp.zeros((1, lon), jnp.int32) for _ in range(4)]
        for v in range(per):
            t = (u * per + v) // erows
            line = (u * per + v) % erows
            d, s, i = (
                meta[t, base + j * erows + line : base + j * erows + line + 1, :] for j in range(3)
            )
            values = (
                t * spec + lax.shift_right_logical(s, shift),
                s & (lon - 1),
                d * spec + lax.shift_right_logical(i, shift),
                i & (lon - 1),
            )
            here = (lanes >= v * width) & (lanes < (v + 1) * width)
            for j in range(4):
                moved = pltpu.roll(values[j], v * width, 1) if v else values[j]
                packed[j] = jnp.where(here, moved, packed[j])
        for j in range(4):
            ent[j, u] = jnp.broadcast_to(packed[j], ent.shape[2:])

    chunk = oh_src.shape[2]
    lines = chunk // lon
    chunks = tiles * entries // chunk
    chunk_tiles = chunk // entries
    crows = chunk_tiles * spec

    def wide(j, c):
        return jnp.concatenate([ent[j, c * lines + v] for v in range(lines)], axis=1)

    def hots(c):
        column = lax.broadcasted_iota(jnp.int32, (lon, chunk), 0)
        one = jnp.where(column == wide(1, c)[0:1, :], 1.0, 0.0).astype(BF16)
        oh_src[c, 0:lon, :] = one
        oh_src[c, lon : 2 * lon, :] = one
        two = jnp.where(column == wide(3, c)[0:1, :], 1.0, 0.0).astype(BF16)
        oh_dst[c, :, 0:chunk] = two
        oh_dst[c, :, chunk : 2 * chunk] = two

    repeat(chunks, hots)
    contract_last = (((1,), (1,)), ((), ()))
    row_block = min(rows, 32)
    for first in range(0, rows, row_block):

        def count(c, total):
            row = lax.broadcasted_iota(jnp.int32, (row_block, chunk), 0) + first
            one = jnp.where(row == wide(2, c)[0:1, :], 1.0, 0.0).astype(BF16)
            return total + lax.dot_general(
                one, oh_dst[c, :, 0:chunk], contract_last, preferred_element_type=F32
            )

        total = lax.fori_loop(0, chunks, count, jnp.zeros((row_block, lon), F32))
        share = 1.0 / (1.0 + total)
        for r in range(row_block):
            inv_b[first + r] = jnp.broadcast_to(share[r : r + 1, :], inv_b.shape[1:])

    def transport(p):
        def substep(step, carry):
            for b in range(pband // 8):
                sub = slice(b * 8, (b + 1) * 8)
                north = speed[0, p, sub, :] > 0
                east = speed[1, p, sub, :] > 0
                zero = jnp.zeros((8, lon), F32)
                current = cells[p, 0, sub, :]
                ahead = cells[p, 1, sub, :]
                prior_diff = current

                def finish(i, value, below, flux, above):
                    t = i // spec
                    value = value - flux + jnp.where(north, below, above)
                    diff = pltpu.roll(value, lon - 1, 1) - value
                    slope = minmod(pltpu.roll(diff, 1, 1), diff)
                    g = coef[2, t, p, sub, :] * value + coef[3, t, p, sub, :] * slope
                    upwind = jnp.where(east, pltpu.roll(g, 1, 1), pltpu.roll(g, lon - 1, 1))
                    cells[p, i, sub, :] = (value - g + upwind) * mask_b[i]

                before, flux, held = zero, None, None
                for i in range(rows):
                    t = i // spec
                    diff = ahead - current
                    slope = minmod(prior_diff, diff)
                    g = coef[0, t, p, sub, :] * current + coef[1, t, p, sub, :] * slope
                    if i > 0:
                        finish(i - 1, held, before, flux, g)
                        before = flux
                    flux, held, prior_diff = g, current, diff
                    current = ahead
                    ahead = cells[p, i + 2, sub, :] if i + 2 < rows else zero
                finish(rows - 1, held, before, flux, zero)
            return carry

        lax.fori_loop(0, SUBSTEPS, substep, 0)

    def nest(p):
        def gather(c):
            x = cells[p, pl.ds(c * crows, crows)].reshape(crows * pband, lon)
            both = jnp.concatenate(split_high_low(x), axis=1)
            picked = jnp.dot(both, oh_src[c], preferred_element_type=F32)
            picked = picked.reshape(crows, pband, chunk)
            home = wide(0, c)[0:1, :] - c * crows
            total = jnp.where(home == 0, picked[0], 0.0)
            for r in range(1, crows):
                total = total + jnp.where(home == r, picked[r], 0.0)
            gathered[c] = total

        repeat(chunks, gather)
        for first in range(0, rows, row_block):

            def scatter(c, total):
                high, low = split_high_low(gathered[c])
                both = jnp.concatenate([high.astype(F32), low.astype(F32)], axis=1)
                home = wide(2, c)[0:1, :]
                home = jnp.concatenate([home, home], axis=1)
                left = [
                    jnp.where(home == first + r, both, 0.0) for r in range(row_block)
                ]
                left = jnp.concatenate(left, axis=0).astype(BF16)
                return total + lax.dot_general(
                    left, oh_dst[c], contract_last, preferred_element_type=F32
                )

            total = jnp.zeros((row_block * pband, lon), F32)
            if chunks <= 4:
                for c in range(chunks):
                    total = scatter(c, total)
            else:
                total = lax.fori_loop(0, chunks, scatter, total)
            total = total.reshape(row_block, pband, lon)
            for r in range(row_block):
                for b in range(pband // 8):
                    sub = slice(b * 8, (b + 1) * 8)
                    cells[p, first + r, sub, :] = (
                        cells[p, first + r, sub, :] + total[r, sub, :]
                    ) * inv_b[first + r]

    def one_part(p, c):
        pltpu.make_async_copy(
            cells.at[p, pl.ds(0, n - 1)], cells.at[p, pl.ds(0, n - 1)], go_recv.at[p]
        ).wait()
        transport(p)
        nest(p)

        def send_back(t, r):
            pltpu.make_async_remote_copy(
                src_ref=cells.at[p, t * spec + r],
                dst_ref=inbox.at[me, p],
                send_sem=back_send.at[p],
                recv_sem=back_recv,
                device_id={"space": t, "spec": r},
                device_id_type=MESH,
            ).start()

        peers(send_back)
        inbox[me, p] = cells[p, me]
        return c

    lax.fori_loop(0, parts, one_part, 0)

    pltpu.make_async_copy(
        inbox.at[pl.ds(0, n - 1)], inbox.at[pl.ds(0, n - 1)], back_recv
    ).wait()
    if band % 8 == 0:
        merged = inbox[...].reshape(bins, lon)
    else:
        for q in range(n):
            field[q * band : (q + 1) * band, :] = inbox[q, 0, 0:band, :]
        merged = field[...]
    out[...] = source(merged) * own_mask

    pltpu.make_async_copy(
        meta.at[pl.ds(0, tiles - 1)], meta.at[pl.ds(0, tiles - 1)], meta_send
    ).wait()
    for p in range(parts):
        sent = outbox.at[pl.ds(0, n - 1), p]
        pltpu.make_async_copy(sent, sent, go_send.at[p]).wait()
        sent = cells.at[p, pl.ds(0, n - 1)]
        pltpu.make_async_copy(sent, sent, back_send.at[p]).wait()


def shards(
    spectra,
    quad_first,
    quad_second,
    quad_output,
    owner_map,
    land_mask,
    nest_dest,
    nest_src,
    nest_into,
):
    spec = lax.axis_size("spec")
    tiles = lax.axis_size("space")
    n = spec * tiles
    bins, _, lon = spectra.shape
    band = bins // n
    parts = PARTS if band % (8 * PARTS) == 0 else 1
    pband = band // parts if band % 8 == 0 else -(-band // 8) * 8
    entries = nest_dest.shape[0]
    width = min(entries, lon)
    erows = entries // width
    meta_rows = -(-(-(-spec // 8) * 8 + 3 * erows) // 8) * 8
    total = tiles * entries
    chunk = max(entries, min(2 * lon, total))
    chunks = total // chunk
    dims = (n, tiles, spec, bins, lon, band, parts, pband, entries)
    vmem = pl.BlockSpec(memory_space=pltpu.VMEM)
    hbm = pl.BlockSpec(memory_space=pltpu.HBM)
    V = pltpu.VMEM
    dma = pltpu.SemaphoreType.DMA
    result = pl.pallas_call(
        functools.partial(kernel, dims),
        out_shape=jax.ShapeDtypeStruct((bins, lon), F32),
        in_specs=[hbm] * 9,
        out_specs=vmem,
        scratch_shapes=[
            pltpu.SMEM(owner_map.shape, jnp.int32),
            V(land_mask.shape, jnp.int32),
            V((erows, width), jnp.int32),
            V((erows, width), jnp.int32),
            V((erows, width), jnp.int32),
            V((bins, lon), F32),
            V(quad_first.shape, BF16),
            V(quad_second.shape, BF16),
            V(quad_output.shape, BF16),
            V((n, parts, pband, lon), F32),
            V((parts, n, pband, lon), F32),
            V((n, parts, pband, lon), F32),
            V((tiles, meta_rows, lon), jnp.int32),
            V((4, total // lon, 8, lon), jnp.int32),
            V((n, 8, lon), F32),
            V((n, 8, lon), F32),
            V((4, tiles, parts, pband, lon), F32),
            V((2, parts, pband, lon), F32),
            V((chunks, 2 * lon, chunk), BF16),
            V((chunks, lon, 2 * chunk), BF16),
            V((chunks, pband, chunk), F32),
            dma((9,)),
            dma,
            dma,
            dma((parts,)),
            dma((parts,)),
            dma((parts,)),
            dma,
        ],
        compiler_params=pltpu.CompilerParams(
            collective_id=0, has_side_effects=True, vmem_limit_bytes=56 * 1024 * 1024
        ),
        cost_estimate=pl.CostEstimate(
            flops=12 * bins * bins * lon, bytes_accessed=6 * bins * bins + 8 * bins * lon, transcendentals=0
        ),
    )(
        spectra.reshape(bins, lon),
        quad_first,
        quad_second,
        quad_output,
        owner_map,
        land_mask,
        nest_dest.reshape(erows, width),
        nest_src.reshape(erows, width),
        nest_into.reshape(erows, width),
    )
    return result.reshape(spectra.shape)


def solution(mesh):
    return jax.shard_map(
        shards,
        mesh=mesh,
        in_specs=(
            P(None, ("space", "spec"), None),
            P(),
            P(),
            P(),
            P(),
            P("space", None),
            P("space"),
            P("space"),
            P("space"),
        ),
        out_specs=P(None, ("space", "spec"), None),
        check_vma=False,
    )
```

```python
import functools
import math

import jax
import jax.numpy as jnp
from jax import lax
from jax.experimental import pallas as pl
from jax.experimental.pallas import tpu as pltpu
from jax.sharding import PartitionSpec as P

DIRS = 24
SUBSTEPS = 6
FREQS = 32
PARTS = 3

step_weight = 0.25
grid_factors = (1.0, 0.55, 0.3)

F32 = jnp.float32
BF16 = jnp.bfloat16
MESH = pl.DeviceIdType.MESH


def minmod(a, b):
    return jnp.maximum(jnp.minimum(a, 0.0), jnp.minimum(b, jnp.maximum(a, 0.0)))


def split_high_low(x):
    high = x.astype(BF16)
    return high, (x - high.astype(F32)).astype(BF16)


def repeat(count, body):
    if count <= 4:
        for i in range(count):
            body(i)
    else:
        lax.fori_loop(0, count, lambda i, c: (body(i), c)[1], 0)


def kernel(
    dims,
    spectra, quad_first, quad_second, quad_output, owner_in, land_in, dest_in, src_in, into_in,
    out, out_mask,
    owner, land, dest, src, into, field, w1, w2, w3, outbox, cells, inbox, sums, meta, ent, mask_b, inv_b, coef, speed, oh_src, oh_dst, gathered,
    load_sem, meta_send, meta_recv, go_send, go_recv, back_send, back_recv,
):
    n, tiles, spec, bins, lon, band, parts, pband, entries = dims
    rows = n
    shift = lon.bit_length() - 1
    spec_rank = lax.axis_index("spec")
    tile = lax.axis_index("space")
    me = tile * spec + spec_rank

    loads = [
        pltpu.make_async_copy(a, b, load_sem.at[i])
        for i, (a, b) in enumerate(
            (
                (land_in, land), (dest_in, dest), (src_in, src), (into_in, into), (owner_in, owner),
                (spectra, field), (quad_first, w1), (quad_second, w2), (quad_output, w3),
            )
        )
    ]
    for copy in loads:
        copy.start()

    def peers(visit):
        def one_tile(j, c):
            offset = tiles // 2 + lax.div(j + 1, 2) * (1 - 2 * lax.rem(j, 2))
            t = tile + offset
            t = jnp.where(t >= tiles, t - tiles, t)
            for k in range(spec):
                r = spec_rank + k
                visit(t, jnp.where(r >= spec, r - spec, r))
            return c

        lax.fori_loop(0, tiles - 1, one_tile, 0)
        for k in range(1, spec):
            r = spec_rank + k
            visit(tile, jnp.where(r >= spec, r - spec, r))

    barrier = pltpu.get_barrier_semaphore()

    def greet(t, r):
        pl.semaphore_signal(
            barrier, inc=1, device_id={"space": t, "spec": r}, device_id_type=MESH
        )

    peers(greet)

    width = min(entries, lon)
    per = lon // width
    erows = entries // width
    base = -(-spec // 8) * 8
    for copy in loads[:5]:
        copy.wait()
    mine = jnp.zeros(meta.shape[1:], jnp.int32)
    meta[tile] = mine
    meta[tile, 0:spec, :] = land[...]
    for j, part in enumerate((dest, src, into)):
        meta[tile, base + j * erows : base + (j + 1) * erows, 0:width] = part[...]
    own_mask = land[pl.ds(spec_rank, 1), :].astype(F32)

    def meta_copy(k):
        return pltpu.make_async_remote_copy(
            src_ref=meta.at[tile],
            dst_ref=meta.at[tile],
            send_sem=meta_send,
            recv_sem=meta_recv,
            device_id={"space": lax.rem(tile + k, tiles), "spec": spec_rank},
            device_id_type=MESH,
        )

    def send_meta(k, c):
        meta_copy(k).start()
        return c

    def third(product, p):
        columns = slice(p * width_p, (p + 1) * width_p)
        return step_weight * jnp.dot(product, w3[:, columns], preferred_element_type=F32).T

    def send_part(p):
        def send(t, r):
            pltpu.make_async_remote_copy(
                src_ref=outbox.at[p, t * spec + r],
                dst_ref=cells.at[p, me],
                send_sem=go_send.at[p],
                recv_sem=go_recv.at[p],
                device_id={"space": t, "spec": r},
                device_id_type=MESH,
            ).start()

        peers(send)
        cells[p, me] = outbox[p, me]

    width_p = bins // parts
    loads[5].wait()
    turned = field[...].T.astype(BF16)
    loads[6].wait()
    one = jnp.dot(turned, w1[...], preferred_element_type=F32)
    loads[7].wait()
    two = jnp.dot(turned, w2[...], preferred_element_type=F32)
    product = (one * two).astype(BF16)
    loads[8].wait()
    pl.semaphore_wait(barrier, n - 1)
    lax.fori_loop(1, tiles, send_meta, 0)
    for p in range(parts):
        sourced = (field[p * width_p : (p + 1) * width_p, :] + third(product, p)) * own_mask
        if band % 8 == 0:
            outbox[p] = sourced.reshape(n, pband, lon)
        else:
            field[...] = sourced
            outbox[...] = jnp.zeros_like(outbox)
            for q in range(n):
                outbox[0, q, 0:band, :] = field[q * band : (q + 1) * band, :]
        send_part(p)

    local = lax.broadcasted_iota(jnp.int32, (parts, pband, lon), 1)
    local = local + lax.broadcasted_iota(jnp.int32, (parts, pband, lon), 0) * width_p
    index = (local + me * (band // parts)).astype(F32)
    freq = jnp.floor((index + 0.5) * (1.0 / DIRS))
    direction = (index - DIRS * freq + 0.5) * (2.0 * math.pi / DIRS)
    speeds = 0.2 + 0.7 * (freq + 0.5) / FREQS
    speed[0] = speeds * jnp.cos(direction)
    speed[1] = speeds * jnp.sin(direction)
    for t in range(tiles):
        grid = owner[t]
        factor = jnp.where(
            grid == 0, grid_factors[0], jnp.where(grid == 1, grid_factors[1], grid_factors[2])
        ).astype(F32)
        for axis in range(2):
            courant = speed[axis] * factor
            coef[2 * axis, t] = jnp.abs(courant)
            coef[2 * axis + 1, t] = 0.5 * courant * (1.0 - jnp.abs(courant))

    drained = pltpu.make_async_copy(
        meta.at[pl.ds(0, tiles - 1)], meta.at[pl.ds(0, tiles - 1)], meta_recv
    )
    drained.wait()
    lanes = lax.broadcasted_iota(jnp.int32, (1, lon), 1)
    for t in range(tiles):
        sea = meta[t, 0:spec, :].astype(F32)
        for r in range(spec):
            mask_b[t * spec + r] = jnp.broadcast_to(sea[r : r + 1, :], mask_b.shape[1:])
    for u in range(tiles * erows // per):
        packed = [jnp.zeros((1, lon), jnp.int32) for _ in range(4)]
        for v in range(per):
            t = (u * per + v) // erows
            line = (u * per + v) % erows
            d, s, i = (
                meta[t, base + j * erows + line : base + j * erows + line + 1, :] for j in range(3)
            )
            values = (
                t * spec + lax.shift_right_logical(s, shift),
                s & (lon - 1),
                d * spec + lax.shift_right_logical(i, shift),
                i & (lon - 1),
            )
            here = (lanes >= v * width) & (lanes < (v + 1) * width)
            for j in range(4):
                moved = pltpu.roll(values[j], v * width, 1) if v else values[j]
                packed[j] = jnp.where(here, moved, packed[j])
        for j in range(4):
            ent[j, u] = jnp.broadcast_to(packed[j], ent.shape[2:])

    chunk = oh_src.shape[2]
    lines = chunk // lon
    chunks = tiles * entries // chunk
    chunk_tiles = chunk // entries
    crows = chunk_tiles * spec

    def wide(j, c):
        return jnp.concatenate([ent[j, c * lines + v] for v in range(lines)], axis=1)

    def hots(c):
        column = lax.broadcasted_iota(jnp.int32, (lon, chunk), 0)
        one = jnp.where(column == wide(1, c)[0:1, :], 1.0, 0.0).astype(BF16)
        oh_src[c, 0:lon, :] = one
        oh_src[c, lon : 2 * lon, :] = one
        two = jnp.where(column == wide(3, c)[0:1, :], 1.0, 0.0).astype(BF16)
        oh_dst[c, :, 0:chunk] = two
        oh_dst[c, :, chunk : 2 * chunk] = two

    repeat(chunks, hots)
    contract_last = (((1,), (1,)), ((), ()))
    row_block = min(rows, 32)
    for first in range(0, rows, row_block):

        def count(c, total):
            row = lax.broadcasted_iota(jnp.int32, (row_block, chunk), 0) + first
            one = jnp.where(row == wide(2, c)[0:1, :], 1.0, 0.0).astype(BF16)
            return total + lax.dot_general(
                one, oh_dst[c, :, 0:chunk], contract_last, preferred_element_type=F32
            )

        total = lax.fori_loop(0, chunks, count, jnp.zeros((row_block, lon), F32))
        share = 1.0 / (1.0 + total)
        for r in range(row_block):
            inv_b[first + r] = jnp.broadcast_to(share[r : r + 1, :], inv_b.shape[1:])

    def transport(p):
        def substep(step, carry):
            for b in range(pband // 8):
                sub = slice(b * 8, (b + 1) * 8)
                north = speed[0, p, sub, :] > 0
                east = speed[1, p, sub, :] > 0
                zero = jnp.zeros((8, lon), F32)
                current = cells[p, 0, sub, :]
                ahead = cells[p, 1, sub, :]
                prior_diff = current

                def finish(i, value, below, flux, above):
                    t = i // spec
                    value = value - flux + jnp.where(north, below, above)
                    diff = pltpu.roll(value, lon - 1, 1) - value
                    slope = minmod(pltpu.roll(diff, 1, 1), diff)
                    g = coef[2, t, p, sub, :] * value + coef[3, t, p, sub, :] * slope
                    upwind = jnp.where(east, pltpu.roll(g, 1, 1), pltpu.roll(g, lon - 1, 1))
                    cells[p, i, sub, :] = (value - g + upwind) * mask_b[i]

                before, flux, held = zero, None, None
                for i in range(rows):
                    t = i // spec
                    diff = ahead - current
                    slope = minmod(prior_diff, diff)
                    g = coef[0, t, p, sub, :] * current + coef[1, t, p, sub, :] * slope
                    if i > 0:
                        finish(i - 1, held, before, flux, g)
                        before = flux
                    flux, held, prior_diff = g, current, diff
                    current = ahead
                    ahead = cells[p, i + 2, sub, :] if i + 2 < rows else zero
                finish(rows - 1, held, before, flux, zero)
            return carry

        lax.fori_loop(0, SUBSTEPS, substep, 0)

    def nest(p):
        def gather(c):
            x = cells[p, pl.ds(c * crows, crows)].reshape(crows * pband, lon)
            both = jnp.concatenate(split_high_low(x), axis=1)
            picked = jnp.dot(both, oh_src[c], preferred_element_type=F32)
            picked = picked.reshape(crows, pband, chunk)
            home = wide(0, c)[0:1, :] - c * crows
            total = jnp.where(home == 0, picked[0], 0.0)
            for r in range(1, crows):
                total = total + jnp.where(home == r, picked[r], 0.0)
            gathered[c] = total

        repeat(chunks, gather)
        for first in range(0, rows, row_block):

            def scatter(c, total):
                high, low = split_high_low(gathered[c])
                both = jnp.concatenate([high.astype(F32), low.astype(F32)], axis=1)
                home = wide(2, c)[0:1, :]
                home = jnp.concatenate([home, home], axis=1)
                left = [
                    jnp.where(home == first + r, both, 0.0) for r in range(row_block)
                ]
                left = jnp.concatenate(left, axis=0).astype(BF16)
                return total + lax.dot_general(
                    left, oh_dst[c], contract_last, preferred_element_type=F32
                )

            total = jnp.zeros((row_block * pband, lon), F32)
            if chunks <= 4:
                for c in range(chunks):
                    total = scatter(c, total)
            else:
                total = lax.fori_loop(0, chunks, scatter, total)
            total = total.reshape(row_block, pband, lon)
            for r in range(row_block):
                for b in range(pband // 8):
                    sub = slice(b * 8, (b + 1) * 8)
                    cells[p, first + r, sub, :] = (
                        cells[p, first + r, sub, :] + total[r, sub, :]
                    ) * inv_b[first + r]

    def one_part(p, c):
        pltpu.make_async_copy(
            cells.at[p, pl.ds(0, n - 1)], cells.at[p, pl.ds(0, n - 1)], go_recv.at[p]
        ).wait()
        transport(p)
        nest(p)

        def send_back(t, r):
            pltpu.make_async_remote_copy(
                src_ref=cells.at[p, t * spec + r],
                dst_ref=inbox.at[p, me],
                send_sem=back_send.at[p],
                recv_sem=back_recv.at[p],
                device_id={"space": t, "spec": r},
                device_id_type=MESH,
            ).start()

        peers(send_back)
        inbox[p, me] = cells[p, me]
        return c

    lax.fori_loop(0, parts, one_part, 0)

    for p in range(parts):
        arrived = inbox.at[p, pl.ds(0, n - 1)]
        pltpu.make_async_copy(arrived, arrived, back_recv.at[p]).wait()
        rows_p = slice(p * width_p, (p + 1) * width_p)
        if band % 8 == 0:
            field[rows_p, :] = inbox[p].reshape(width_p, lon)
        else:
            for q in range(n):
                field[q * band : (q + 1) * band, :] = inbox[0, q, 0:band, :]
        turned = field[rows_p, :].T.astype(BF16)
        one = jnp.dot(turned, w1[rows_p, :], preferred_element_type=F32)
        two = jnp.dot(turned, w2[rows_p, :], preferred_element_type=F32)
        if p > 0:
            one = one + sums[0]
            two = two + sums[1]
        if p < parts - 1:
            sums[0] = one
            sums[1] = two
    product = (one * two).astype(BF16)
    for p in range(parts):
        rows_p = slice(p * width_p, (p + 1) * width_p)
        out[rows_p, :] = field[rows_p, :] + third(product, p)
    out_mask[...] = own_mask

    pltpu.make_async_copy(
        meta.at[pl.ds(0, tiles - 1)], meta.at[pl.ds(0, tiles - 1)], meta_send
    ).wait()
    for p in range(parts):
        sent = outbox.at[p, pl.ds(0, n - 1)]
        pltpu.make_async_copy(sent, sent, go_send.at[p]).wait()
        sent = cells.at[p, pl.ds(0, n - 1)]
        pltpu.make_async_copy(sent, sent, back_send.at[p]).wait()


def shards(
    spectra,
    quad_first,
    quad_second,
    quad_output,
    owner_map,
    land_mask,
    nest_dest,
    nest_src,
    nest_into,
):
    spec = lax.axis_size("spec")
    tiles = lax.axis_size("space")
    n = spec * tiles
    bins, _, lon = spectra.shape
    band = bins // n
    parts = PARTS if band % (8 * PARTS) == 0 else 1
    pband = band // parts if band % 8 == 0 else -(-band // 8) * 8
    entries = nest_dest.shape[0]
    width = min(entries, lon)
    erows = entries // width
    meta_rows = -(-(-(-spec // 8) * 8 + 3 * erows) // 8) * 8
    total = tiles * entries
    chunk = max(entries, min(2 * lon, total))
    chunks = total // chunk
    dims = (n, tiles, spec, bins, lon, band, parts, pband, entries)
    vmem = pl.BlockSpec(memory_space=pltpu.VMEM)
    hbm = pl.BlockSpec(memory_space=pltpu.HBM)
    V = pltpu.VMEM
    dma = pltpu.SemaphoreType.DMA
    result, own_row = pl.pallas_call(
        functools.partial(kernel, dims),
        out_shape=[jax.ShapeDtypeStruct((bins, lon), F32), jax.ShapeDtypeStruct((1, lon), F32)],
        in_specs=[hbm] * 9,
        out_specs=[vmem, vmem],
        scratch_shapes=[
            pltpu.SMEM(owner_map.shape, jnp.int32),
            V(land_mask.shape, jnp.int32),
            V((erows, width), jnp.int32),
            V((erows, width), jnp.int32),
            V((erows, width), jnp.int32),
            V((bins, lon), F32),
            V(quad_first.shape, BF16),
            V(quad_second.shape, BF16),
            V(quad_output.shape, BF16),
            V((parts, n, pband, lon), F32),
            V((parts, n, pband, lon), F32),
            V((parts, n, pband, lon), F32),
            V((2, lon, bins), F32),
            V((tiles, meta_rows, lon), jnp.int32),
            V((4, total // lon, 8, lon), jnp.int32),
            V((n, 8, lon), F32),
            V((n, 8, lon), F32),
            V((4, tiles, parts, pband, lon), F32),
            V((2, parts, pband, lon), F32),
            V((chunks, 2 * lon, chunk), BF16),
            V((chunks, lon, 2 * chunk), BF16),
            V((chunks, pband, chunk), F32),
            dma((9,)),
            dma,
            dma,
            dma((parts,)),
            dma((parts,)),
            dma((parts,)),
            dma((parts,)),
        ],
        compiler_params=pltpu.CompilerParams(
            collective_id=0, has_side_effects=True, vmem_limit_bytes=56 * 1024 * 1024
        ),
        cost_estimate=pl.CostEstimate(
            flops=12 * bins * bins * lon, bytes_accessed=6 * bins * bins + 8 * bins * lon, transcendentals=0
        ),
    )(
        spectra.reshape(bins, lon),
        quad_first,
        quad_second,
        quad_output,
        owner_map,
        land_mask,
        nest_dest.reshape(erows, width),
        nest_src.reshape(erows, width),
        nest_into.reshape(erows, width),
    )
    return (result * own_row).reshape(spectra.shape)


def solution(mesh):
    return jax.shard_map(
        shards,
        mesh=mesh,
        in_specs=(
            P(None, ("space", "spec"), None),
            P(),
            P(),
            P(),
            P(),
            P("space", None),
            P("space"),
            P("space"),
            P("space"),
        ),
        out_specs=P(None, ("space", "spec"), None),
        check_vma=False,
    )
```

```python
import functools
import math

import jax
import jax.numpy as jnp
from jax import lax
from jax.experimental import pallas as pl
from jax.experimental.pallas import tpu as pltpu
from jax.sharding import PartitionSpec as P

DIRS = 24
SUBSTEPS = 6
FREQS = 32
PARTS = 3

step_weight = 0.25
grid_factors = (1.0, 0.55, 0.3)

F32 = jnp.float32
BF16 = jnp.bfloat16
MESH = pl.DeviceIdType.MESH


def minmod(a, b):
    return jnp.maximum(jnp.minimum(a, 0.0), jnp.minimum(b, jnp.maximum(a, 0.0)))


def split_high_low(x):
    high = x.astype(BF16)
    return high, (x - high.astype(F32)).astype(BF16)


def repeat(count, body):
    if count <= 4:
        for i in range(count):
            body(i)
    else:
        lax.fori_loop(0, count, lambda i, c: (body(i), c)[1], 0)


def kernel(
    dims,
    spectra, quad_first, quad_second, quad_output, owner_in, land_in, dest_in, src_in, into_in,
    out, out_mask,
    owner, land, dest, src, into, field, w1, w2, w3, outbox, cells, inbox, sums, meta, ent, mask_b, inv_b, coef, speed, oh_src, oh_dst, gathered,
    load_sem, meta_send, meta_recv, go_send, go_recv, back_send, back_recv,
):
    n, tiles, spec, bins, lon, band, parts, pband, entries = dims
    rows = n
    shift = lon.bit_length() - 1
    spec_rank = lax.axis_index("spec")
    tile = lax.axis_index("space")
    me = tile * spec + spec_rank

    loads = [
        pltpu.make_async_copy(a, b, load_sem.at[i])
        for i, (a, b) in enumerate(
            (
                (land_in, land), (dest_in, dest), (src_in, src), (into_in, into), (owner_in, owner),
                (spectra, field), (quad_first, w1), (quad_second, w2), (quad_output, w3),
            )
        )
    ]
    for copy in loads:
        copy.start()

    def peers(visit):
        def one_tile(j, c):
            offset = tiles // 2 + lax.div(j + 1, 2) * (1 - 2 * lax.rem(j, 2))
            t = tile + offset
            t = jnp.where(t >= tiles, t - tiles, t)
            for k in range(spec):
                r = spec_rank + k
                visit(t, jnp.where(r >= spec, r - spec, r))
            return c

        lax.fori_loop(0, tiles - 1, one_tile, 0)
        for k in range(1, spec):
            r = spec_rank + k
            visit(tile, jnp.where(r >= spec, r - spec, r))

    barrier = pltpu.get_barrier_semaphore()

    def greet(t, r):
        pl.semaphore_signal(
            barrier, inc=1, device_id={"space": t, "spec": r}, device_id_type=MESH
        )

    peers(greet)

    width = min(entries, lon)
    per = lon // width
    erows = entries // width
    base = -(-spec // 8) * 8
    for copy in loads[:5]:
        copy.wait()
    mine = jnp.zeros(meta.shape[1:], jnp.int32)
    meta[tile] = mine
    meta[tile, 0:spec, :] = land[...]
    for j, part in enumerate((dest, src, into)):
        meta[tile, base + j * erows : base + (j + 1) * erows, 0:width] = part[...]
    own_mask = land[pl.ds(spec_rank, 1), :].astype(F32)

    def meta_copy(k):
        return pltpu.make_async_remote_copy(
            src_ref=meta.at[tile],
            dst_ref=meta.at[tile],
            send_sem=meta_send,
            recv_sem=meta_recv,
            device_id={"space": lax.rem(tile + k, tiles), "spec": spec_rank},
            device_id_type=MESH,
        )

    def send_meta(k, c):
        meta_copy(k).start()
        return c

    def third(product, p):
        columns = slice(p * width_p, (p + 1) * width_p)
        return step_weight * jnp.dot(product, w3[:, columns], preferred_element_type=F32).T

    def send_part(p):
        def send(t, r):
            pltpu.make_async_remote_copy(
                src_ref=outbox.at[p, t * spec + r],
                dst_ref=cells.at[p, me],
                send_sem=go_send.at[p],
                recv_sem=go_recv.at[p],
                device_id={"space": t, "spec": r},
                device_id_type=MESH,
            ).start()

        peers(send)
        cells[p, me] = outbox[p, me]

    width_p = bins // parts
    local = lax.broadcasted_iota(jnp.int32, (parts, pband, lon), 1)
    local = local + lax.broadcasted_iota(jnp.int32, (parts, pband, lon), 0) * width_p
    index = (local + me * (band // parts)).astype(F32)
    freq = jnp.floor((index + 0.5) * (1.0 / DIRS))
    direction = (index - DIRS * freq + 0.5) * (2.0 * math.pi / DIRS)
    speeds = 0.2 + 0.7 * (freq + 0.5) / FREQS
    speed[0] = speeds * jnp.cos(direction)
    speed[1] = speeds * jnp.sin(direction)
    for t in range(tiles):
        grid = owner[t]
        factor = jnp.where(
            grid == 0, grid_factors[0], jnp.where(grid == 1, grid_factors[1], grid_factors[2])
        ).astype(F32)
        for axis in range(2):
            courant = speed[axis] * factor
            coef[2 * axis, t] = jnp.abs(courant)
            coef[2 * axis + 1, t] = 0.5 * courant * (1.0 - jnp.abs(courant))

    loads[5].wait()
    turned = field[...].T.astype(BF16)
    loads[6].wait()
    one = jnp.dot(turned, w1[...], preferred_element_type=F32)
    loads[7].wait()
    two = jnp.dot(turned, w2[...], preferred_element_type=F32)
    product = (one * two).astype(BF16)
    loads[8].wait()
    pl.semaphore_wait(barrier, n - 1)
    lax.fori_loop(1, tiles, send_meta, 0)
    for p in range(parts):
        sourced = (field[p * width_p : (p + 1) * width_p, :] + third(product, p)) * own_mask
        if band % 8 == 0:
            outbox[p] = sourced.reshape(n, pband, lon)
        else:
            field[...] = sourced
            outbox[...] = jnp.zeros_like(outbox)
            for q in range(n):
                outbox[0, q, 0:band, :] = field[q * band : (q + 1) * band, :]
        send_part(p)

    drained = pltpu.make_async_copy(
        meta.at[pl.ds(0, tiles - 1)], meta.at[pl.ds(0, tiles - 1)], meta_recv
    )
    drained.wait()
    lanes = lax.broadcasted_iota(jnp.int32, (1, lon), 1)
    for t in range(tiles):
        sea = meta[t, 0:spec, :].astype(F32)
        for r in range(spec):
            mask_b[t * spec + r] = jnp.broadcast_to(sea[r : r + 1, :], mask_b.shape[1:])
    for u in range(tiles * erows // per):
        packed = [jnp.zeros((1, lon), jnp.int32) for _ in range(4)]
        for v in range(per):
            t = (u * per + v) // erows
            line = (u * per + v) % erows
            d, s, i = (
                meta[t, base + j * erows + line : base + j * erows + line + 1, :] for j in range(3)
            )
            values = (
                t * spec + lax.shift_right_logical(s, shift),
                s & (lon - 1),
                d * spec + lax.shift_right_logical(i, shift),
                i & (lon - 1),
            )
            here = (lanes >= v * width) & (lanes < (v + 1) * width)
            for j in range(4):
                moved = pltpu.roll(values[j], v * width, 1) if v else values[j]
                packed[j] = jnp.where(here, moved, packed[j])
        for j in range(4):
            ent[j, u] = jnp.broadcast_to(packed[j], ent.shape[2:])

    chunk = oh_src.shape[2]
    lines = chunk // lon
    chunks = tiles * entries // chunk
    chunk_tiles = chunk // entries
    crows = chunk_tiles * spec

    def wide(j, c):
        return jnp.concatenate([ent[j, c * lines + v] for v in range(lines)], axis=1)

    def hots(c):
        column = lax.broadcasted_iota(jnp.int32, (lon, chunk), 0)
        one = jnp.where(column == wide(1, c)[0:1, :], 1.0, 0.0).astype(BF16)
        oh_src[c, 0:lon, :] = one
        oh_src[c, lon : 2 * lon, :] = one
        two = jnp.where(column == wide(3, c)[0:1, :], 1.0, 0.0).astype(BF16)
        oh_dst[c, :, 0:chunk] = two
        oh_dst[c, :, chunk : 2 * chunk] = two

    repeat(chunks, hots)
    contract_last = (((1,), (1,)), ((), ()))
    row_block = min(rows, 32)
    for first in range(0, rows, row_block):

        def count(c, total):
            row = lax.broadcasted_iota(jnp.int32, (row_block, chunk), 0) + first
            one = jnp.where(row == wide(2, c)[0:1, :], 1.0, 0.0).astype(BF16)
            return total + lax.dot_general(
                one, oh_dst[c, :, 0:chunk], contract_last, preferred_element_type=F32
            )

        total = lax.fori_loop(0, chunks, count, jnp.zeros((row_block, lon), F32))
        share = 1.0 / (1.0 + total)
        for r in range(row_block):
            inv_b[first + r] = jnp.broadcast_to(share[r : r + 1, :], inv_b.shape[1:])

    def substep(p, sub, values):
        north = speed[0, p, sub, :] > 0
        east = speed[1, p, sub, :] > 0
        zero = jnp.zeros((8, lon), F32)

        def along_row(i, value, flux, below, above):
            t = i // spec
            value = value - flux + jnp.where(north, below, above)
            diff = pltpu.roll(value, lon - 1, 1) - value
            slope = minmod(pltpu.roll(diff, 1, 1), diff)
            g = coef[2, t, p, sub, :] * value + coef[3, t, p, sub, :] * slope
            upwind = jnp.where(east, pltpu.roll(g, 1, 1), pltpu.roll(g, lon - 1, 1))
            return (value - g + upwind) * mask_b[i]

        below, flux, held = zero, None, None
        current = next(values)
        prior = current
        for i in range(rows):
            t = i // spec
            ahead = next(values) if i + 1 < rows else zero
            diff = ahead - current
            g = coef[0, t, p, sub, :] * current + coef[1, t, p, sub, :] * minmod(prior, diff)
            if i > 0:
                yield along_row(i - 1, held, flux, below, g)
                below = flux
            flux, held, prior, current = g, current, diff, ahead
        yield along_row(rows - 1, held, flux, below, zero)

    def stream(p, sub, count):
        values = (cells[p, i, sub, :] for i in range(rows))
        for _ in range(count):
            values = substep(p, sub, values)
        for i, value in enumerate(values):
            cells[p, i, sub, :] = value

    def transport(p):
        count = SUBSTEPS if rows <= 64 else 1
        for b in range(pband // 8):
            sub = slice(b * 8, (b + 1) * 8)

            def chain(step, carry):
                stream(p, sub, count)
                return carry

            if count == SUBSTEPS:
                chain(0, 0)
            else:
                lax.fori_loop(0, SUBSTEPS, chain, 0)

    def nest(p):
        def gather(c):
            x = cells[p, pl.ds(c * crows, crows)].reshape(crows * pband, lon)
            both = jnp.concatenate(split_high_low(x), axis=1)
            picked = jnp.dot(both, oh_src[c], preferred_element_type=F32)
            picked = picked.reshape(crows, pband, chunk)
            home = wide(0, c)[0:1, :] - c * crows
            total = jnp.where(home == 0, picked[0], 0.0)
            for r in range(1, crows):
                total = total + jnp.where(home == r, picked[r], 0.0)
            gathered[c] = total

        repeat(chunks, gather)
        for first in range(0, rows, row_block):

            def scatter(c, total):
                high, low = split_high_low(gathered[c])
                both = jnp.concatenate([high.astype(F32), low.astype(F32)], axis=1)
                home = wide(2, c)[0:1, :]
                home = jnp.concatenate([home, home], axis=1)
                left = [
                    jnp.where(home == first + r, both, 0.0) for r in range(row_block)
                ]
                left = jnp.concatenate(left, axis=0).astype(BF16)
                return total + lax.dot_general(
                    left, oh_dst[c], contract_last, preferred_element_type=F32
                )

            total = jnp.zeros((row_block * pband, lon), F32)
            if chunks <= 4:
                for c in range(chunks):
                    total = scatter(c, total)
            else:
                total = lax.fori_loop(0, chunks, scatter, total)
            total = total.reshape(row_block, pband, lon)
            for r in range(row_block):
                for b in range(pband // 8):
                    sub = slice(b * 8, (b + 1) * 8)
                    cells[p, first + r, sub, :] = (
                        cells[p, first + r, sub, :] + total[r, sub, :]
                    ) * inv_b[first + r]

    def one_part(p, c):
        pltpu.make_async_copy(
            cells.at[p, pl.ds(0, n - 1)], cells.at[p, pl.ds(0, n - 1)], go_recv.at[p]
        ).wait()
        transport(p)
        nest(p)

        def send_back(t, r):
            pltpu.make_async_remote_copy(
                src_ref=cells.at[p, t * spec + r],
                dst_ref=inbox.at[p, me],
                send_sem=back_send.at[p],
                recv_sem=back_recv.at[p],
                device_id={"space": t, "spec": r},
                device_id_type=MESH,
            ).start()

        peers(send_back)
        inbox[p, me] = cells[p, me]
        return c

    lax.fori_loop(0, parts, one_part, 0)

    for p in range(parts):
        arrived = inbox.at[p, pl.ds(0, n - 1)]
        pltpu.make_async_copy(arrived, arrived, back_recv.at[p]).wait()
        rows_p = slice(p * width_p, (p + 1) * width_p)
        if band % 8 == 0:
            field[rows_p, :] = inbox[p].reshape(width_p, lon)
        else:
            for q in range(n):
                field[q * band : (q + 1) * band, :] = inbox[0, q, 0:band, :]
        turned = field[rows_p, :].T.astype(BF16)
        one = jnp.dot(turned, w1[rows_p, :], preferred_element_type=F32)
        two = jnp.dot(turned, w2[rows_p, :], preferred_element_type=F32)
        if p > 0:
            one = one + sums[0]
            two = two + sums[1]
        if p < parts - 1:
            sums[0] = one
            sums[1] = two
    product = (one * two).astype(BF16)
    for p in range(parts):
        rows_p = slice(p * width_p, (p + 1) * width_p)
        out[rows_p, :] = field[rows_p, :] + third(product, p)
    out_mask[...] = own_mask

    pltpu.make_async_copy(
        meta.at[pl.ds(0, tiles - 1)], meta.at[pl.ds(0, tiles - 1)], meta_send
    ).wait()
    for p in range(parts):
        sent = outbox.at[p, pl.ds(0, n - 1)]
        pltpu.make_async_copy(sent, sent, go_send.at[p]).wait()
        sent = cells.at[p, pl.ds(0, n - 1)]
        pltpu.make_async_copy(sent, sent, back_send.at[p]).wait()


def masked(value, mask, out):
    out[...] = value[...] * mask[...]


def shards(
    spectra,
    quad_first,
    quad_second,
    quad_output,
    owner_map,
    land_mask,
    nest_dest,
    nest_src,
    nest_into,
):
    spec = lax.axis_size("spec")
    tiles = lax.axis_size("space")
    n = spec * tiles
    bins, _, lon = spectra.shape
    band = bins // n
    parts = PARTS if band % (8 * PARTS) == 0 else 1
    pband = band // parts if band % 8 == 0 else -(-band // 8) * 8
    entries = nest_dest.shape[0]
    width = min(entries, lon)
    erows = entries // width
    meta_rows = -(-(-(-spec // 8) * 8 + 3 * erows) // 8) * 8
    total = tiles * entries
    chunk = max(entries, min(2 * lon, total))
    chunks = total // chunk
    dims = (n, tiles, spec, bins, lon, band, parts, pband, entries)
    vmem = pl.BlockSpec(memory_space=pltpu.VMEM)
    hbm = pl.BlockSpec(memory_space=pltpu.HBM)
    V = pltpu.VMEM
    dma = pltpu.SemaphoreType.DMA
    result, own_row = pl.pallas_call(
        functools.partial(kernel, dims),
        out_shape=[jax.ShapeDtypeStruct((bins, lon), F32), jax.ShapeDtypeStruct((1, lon), F32)],
        in_specs=[hbm] * 9,
        out_specs=[vmem, vmem],
        scratch_shapes=[
            pltpu.SMEM(owner_map.shape, jnp.int32),
            V(land_mask.shape, jnp.int32),
            V((erows, width), jnp.int32),
            V((erows, width), jnp.int32),
            V((erows, width), jnp.int32),
            V((bins, lon), F32),
            V(quad_first.shape, BF16),
            V(quad_second.shape, BF16),
            V(quad_output.shape, BF16),
            V((parts, n, pband, lon), F32),
            V((parts, n, pband, lon), F32),
            V((parts, n, pband, lon), F32),
            V((2, lon, bins), F32),
            V((tiles, meta_rows, lon), jnp.int32),
            V((4, total // lon, 8, lon), jnp.int32),
            V((n, 8, lon), F32),
            V((n, 8, lon), F32),
            V((4, tiles, parts, pband, lon), F32),
            V((2, parts, pband, lon), F32),
            V((chunks, 2 * lon, chunk), BF16),
            V((chunks, lon, 2 * chunk), BF16),
            V((chunks, pband, chunk), F32),
            dma((9,)),
            dma,
            dma,
            dma((parts,)),
            dma((parts,)),
            dma((parts,)),
            dma((parts,)),
        ],
        compiler_params=pltpu.CompilerParams(
            collective_id=0, has_side_effects=True, vmem_limit_bytes=56 * 1024 * 1024
        ),
        cost_estimate=pl.CostEstimate(
            flops=12 * bins * bins * lon, bytes_accessed=6 * bins * bins + 8 * bins * lon, transcendentals=0
        ),
    )(
        spectra.reshape(bins, lon),
        quad_first,
        quad_second,
        quad_output,
        owner_map,
        land_mask,
        nest_dest.reshape(erows, width),
        nest_src.reshape(erows, width),
        nest_into.reshape(erows, width),
    )
    blocks = 3 if bins % 24 == 0 else 1
    block = pl.BlockSpec((bins // blocks, lon), lambda i: (i, 0))
    return pl.pallas_call(
        masked,
        grid=(blocks,),
        out_shape=jax.ShapeDtypeStruct((bins, lon), F32),
        in_specs=[block, pl.BlockSpec((1, lon), lambda i: (0, 0))],
        out_specs=block,
        compiler_params=pltpu.CompilerParams(vmem_limit_bytes=56 * 1024 * 1024),
    )(result, own_row).reshape(spectra.shape)


def solution(mesh):
    return jax.shard_map(
        shards,
        mesh=mesh,
        in_specs=(
            P(None, ("space", "spec"), None),
            P(),
            P(),
            P(),
            P(),
            P("space", None),
            P("space"),
            P("space"),
            P("space"),
        ),
        out_specs=P(None, ("space", "spec"), None),
        check_vma=False,
    )
```

```python
import functools
import math

import jax
import jax.numpy as jnp
from jax import lax
from jax.experimental import pallas as pl
from jax.experimental.pallas import tpu as pltpu
from jax.sharding import PartitionSpec as P

DIRS = 24
SUBSTEPS = 6
FREQS = 32
PARTS = 3

step_weight = 0.25
grid_factors = (1.0, 0.55, 0.3)

F32 = jnp.float32
BF16 = jnp.bfloat16
MESH = pl.DeviceIdType.MESH


def minmod(a, b):
    return jnp.maximum(jnp.minimum(a, 0.0), jnp.minimum(b, jnp.maximum(a, 0.0)))


def split_high_low(x):
    high = x.astype(BF16)
    return high, (x - high.astype(F32)).astype(BF16)


def repeat(count, body):
    if count <= 4:
        for i in range(count):
            body(i)
    else:
        lax.fori_loop(0, count, lambda i, c: (body(i), c)[1], 0)


def kernel(
    dims,
    spectra, quad_first, quad_second, quad_output, owner_in, land_in, dest_in, src_in, into_in,
    out,
    owner, land, dest, src, into, field, w1, w2, w3, outbox, cells, inbox, sums, meta, ent, mask_b, inv_b, coef, speed, oh_src, oh_dst, gathered,
    load_sem, meta_send, meta_recv, go_send, go_recv, back_send, back_recv,
):
    n, tiles, spec, bins, lon, band, parts, pband, entries = dims
    rows = n
    shift = lon.bit_length() - 1
    spec_rank = lax.axis_index("spec")
    tile = lax.axis_index("space")
    me = tile * spec + spec_rank

    loads = [
        pltpu.make_async_copy(a, b, load_sem.at[i])
        for i, (a, b) in enumerate(
            (
                (land_in, land), (dest_in, dest), (src_in, src), (into_in, into), (owner_in, owner),
                (spectra, field), (quad_first, w1), (quad_second, w2), (quad_output, w3),
            )
        )
    ]
    for copy in loads:
        copy.start()

    def peers(visit):
        def one_tile(j, c):
            offset = tiles // 2 + lax.div(j + 1, 2) * (1 - 2 * lax.rem(j, 2))
            t = tile + offset
            t = jnp.where(t >= tiles, t - tiles, t)
            for k in range(spec):
                r = spec_rank + k
                visit(t, jnp.where(r >= spec, r - spec, r))
            return c

        lax.fori_loop(0, tiles - 1, one_tile, 0)
        for k in range(1, spec):
            r = spec_rank + k
            visit(tile, jnp.where(r >= spec, r - spec, r))

    barrier = pltpu.get_barrier_semaphore()

    def greet(t, r):
        pl.semaphore_signal(
            barrier, inc=1, device_id={"space": t, "spec": r}, device_id_type=MESH
        )

    peers(greet)

    width = min(entries, lon)
    per = lon // width
    erows = entries // width
    base = -(-spec // 8) * 8
    for copy in loads[:5]:
        copy.wait()
    mine = jnp.zeros(meta.shape[1:], jnp.int32)
    meta[tile] = mine
    meta[tile, 0:spec, :] = land[...]
    for j, part in enumerate((dest, src, into)):
        meta[tile, base + j * erows : base + (j + 1) * erows, 0:width] = part[...]
    own_mask = land[pl.ds(spec_rank, 1), :].astype(F32)

    def meta_copy(k):
        return pltpu.make_async_remote_copy(
            src_ref=meta.at[tile],
            dst_ref=meta.at[tile],
            send_sem=meta_send,
            recv_sem=meta_recv,
            device_id={"space": lax.rem(tile + k, tiles), "spec": spec_rank},
            device_id_type=MESH,
        )

    def send_meta(k, c):
        meta_copy(k).start()
        return c

    def third(product, p):
        columns = slice(p * width_p, (p + 1) * width_p)
        return step_weight * jnp.dot(product, w3[:, columns], preferred_element_type=F32).T

    def send_part(p):
        def send(t, r):
            pltpu.make_async_remote_copy(
                src_ref=outbox.at[p, t * spec + r],
                dst_ref=cells.at[p, me],
                send_sem=go_send.at[p],
                recv_sem=go_recv.at[p],
                device_id={"space": t, "spec": r},
                device_id_type=MESH,
            ).start()

        peers(send)
        cells[p, me] = outbox[p, me]

    width_p = bins // parts
    local = lax.broadcasted_iota(jnp.int32, (parts, pband, lon), 1)
    local = local + lax.broadcasted_iota(jnp.int32, (parts, pband, lon), 0) * width_p
    index = (local + me * (band // parts)).astype(F32)
    freq = jnp.floor((index + 0.5) * (1.0 / DIRS))
    direction = (index - DIRS * freq + 0.5) * (2.0 * math.pi / DIRS)
    speeds = 0.2 + 0.7 * (freq + 0.5) / FREQS
    speed[0] = speeds * jnp.cos(direction)
    speed[1] = speeds * jnp.sin(direction)
    for t in range(tiles):
        grid = owner[t]
        factor = jnp.where(
            grid == 0, grid_factors[0], jnp.where(grid == 1, grid_factors[1], grid_factors[2])
        ).astype(F32)
        for axis in range(2):
            courant = speed[axis] * factor
            coef[2 * axis, t] = jnp.abs(courant)
            coef[2 * axis + 1, t] = 0.5 * courant * (1.0 - jnp.abs(courant))

    loads[5].wait()
    turned = field[...].T.astype(BF16)
    loads[6].wait()
    one = jnp.dot(turned, w1[...], preferred_element_type=F32)
    loads[7].wait()
    two = jnp.dot(turned, w2[...], preferred_element_type=F32)
    product = (one * two).astype(BF16)
    loads[8].wait()
    pl.semaphore_wait(barrier, n - 1)
    lax.fori_loop(1, tiles, send_meta, 0)
    for p in range(parts):
        sourced = (field[p * width_p : (p + 1) * width_p, :] + third(product, p)) * own_mask
        if band % 8 == 0:
            outbox[p] = sourced.reshape(n, pband, lon)
        else:
            field[...] = sourced
            outbox[...] = jnp.zeros_like(outbox)
            for q in range(n):
                outbox[0, q, 0:band, :] = field[q * band : (q + 1) * band, :]
        send_part(p)

    drained = pltpu.make_async_copy(
        meta.at[pl.ds(0, tiles - 1)], meta.at[pl.ds(0, tiles - 1)], meta_recv
    )
    drained.wait()
    lanes = lax.broadcasted_iota(jnp.int32, (1, lon), 1)
    for t in range(tiles):
        sea = meta[t, 0:spec, :].astype(F32)
        for r in range(spec):
            mask_b[t * spec + r] = jnp.broadcast_to(sea[r : r + 1, :], mask_b.shape[1:])
    for u in range(tiles * erows // per):
        packed = [jnp.zeros((1, lon), jnp.int32) for _ in range(4)]
        for v in range(per):
            t = (u * per + v) // erows
            line = (u * per + v) % erows
            d, s, i = (
                meta[t, base + j * erows + line : base + j * erows + line + 1, :] for j in range(3)
            )
            values = (
                t * spec + lax.shift_right_logical(s, shift),
                s & (lon - 1),
                d * spec + lax.shift_right_logical(i, shift),
                i & (lon - 1),
            )
            here = (lanes >= v * width) & (lanes < (v + 1) * width)
            for j in range(4):
                moved = pltpu.roll(values[j], v * width, 1) if v else values[j]
                packed[j] = jnp.where(here, moved, packed[j])
        for j in range(4):
            ent[j, u] = jnp.broadcast_to(packed[j], ent.shape[2:])

    chunk = oh_src.shape[2]
    lines = chunk // lon
    chunks = tiles * entries // chunk
    chunk_tiles = chunk // entries
    crows = chunk_tiles * spec

    def wide(j, c):
        return jnp.concatenate([ent[j, c * lines + v] for v in range(lines)], axis=1)

    def hots(c):
        column = lax.broadcasted_iota(jnp.int32, (lon, chunk), 0)
        one = jnp.where(column == wide(1, c)[0:1, :], 1.0, 0.0).astype(BF16)
        oh_src[c, 0:lon, :] = one
        oh_src[c, lon : 2 * lon, :] = one
        two = jnp.where(column == wide(3, c)[0:1, :], 1.0, 0.0).astype(BF16)
        oh_dst[c, :, 0:chunk] = two
        oh_dst[c, :, chunk : 2 * chunk] = two

    repeat(chunks, hots)
    contract_last = (((1,), (1,)), ((), ()))
    row_block = min(rows, 32)
    for first in range(0, rows, row_block):

        def count(c, total):
            row = lax.broadcasted_iota(jnp.int32, (row_block, chunk), 0) + first
            one = jnp.where(row == wide(2, c)[0:1, :], 1.0, 0.0).astype(BF16)
            return total + lax.dot_general(
                one, oh_dst[c, :, 0:chunk], contract_last, preferred_element_type=F32
            )

        total = lax.fori_loop(0, chunks, count, jnp.zeros((row_block, lon), F32))
        share = 1.0 / (1.0 + total)
        for r in range(row_block):
            inv_b[first + r] = jnp.broadcast_to(share[r : r + 1, :], inv_b.shape[1:])

    def substep(p, sub, values):
        north = speed[0, p, sub, :] > 0
        east = speed[1, p, sub, :] > 0
        zero = jnp.zeros((8, lon), F32)

        def along_row(i, value, flux, below, above):
            t = i // spec
            value = value - flux + jnp.where(north, below, above)
            diff = pltpu.roll(value, lon - 1, 1) - value
            slope = minmod(pltpu.roll(diff, 1, 1), diff)
            g = coef[2, t, p, sub, :] * value + coef[3, t, p, sub, :] * slope
            upwind = jnp.where(east, pltpu.roll(g, 1, 1), pltpu.roll(g, lon - 1, 1))
            return (value - g + upwind) * mask_b[i]

        below, flux, held = zero, None, None
        current = next(values)
        prior = current
        for i in range(rows):
            t = i // spec
            ahead = next(values) if i + 1 < rows else zero
            diff = ahead - current
            g = coef[0, t, p, sub, :] * current + coef[1, t, p, sub, :] * minmod(prior, diff)
            if i > 0:
                yield along_row(i - 1, held, flux, below, g)
                below = flux
            flux, held, prior, current = g, current, diff, ahead
        yield along_row(rows - 1, held, flux, below, zero)

    def stream(p, sub, count):
        values = (cells[p, i, sub, :] for i in range(rows))
        for _ in range(count):
            values = substep(p, sub, values)
        for i, value in enumerate(values):
            cells[p, i, sub, :] = value

    def transport(p):
        count = SUBSTEPS if rows <= 64 else 1
        for b in range(pband // 8):
            sub = slice(b * 8, (b + 1) * 8)

            def chain(step, carry):
                stream(p, sub, count)
                return carry

            if count == SUBSTEPS:
                chain(0, 0)
            else:
                lax.fori_loop(0, SUBSTEPS, chain, 0)

    def nest(p):
        def gather(c):
            x = cells[p, pl.ds(c * crows, crows)].reshape(crows * pband, lon)
            both = jnp.concatenate(split_high_low(x), axis=1)
            picked = jnp.dot(both, oh_src[c], preferred_element_type=F32)
            picked = picked.reshape(crows, pband, chunk)
            home = wide(0, c)[0:1, :] - c * crows
            total = jnp.where(home == 0, picked[0], 0.0)
            for r in range(1, crows):
                total = total + jnp.where(home == r, picked[r], 0.0)
            gathered[c] = total

        repeat(chunks, gather)
        for first in range(0, rows, row_block):

            def scatter(c, total):
                high, low = split_high_low(gathered[c])
                both = jnp.concatenate([high.astype(F32), low.astype(F32)], axis=1)
                home = wide(2, c)[0:1, :]
                home = jnp.concatenate([home, home], axis=1)
                left = [
                    jnp.where(home == first + r, both, 0.0) for r in range(row_block)
                ]
                left = jnp.concatenate(left, axis=0).astype(BF16)
                return total + lax.dot_general(
                    left, oh_dst[c], contract_last, preferred_element_type=F32
                )

            total = jnp.zeros((row_block * pband, lon), F32)
            if chunks <= 4:
                for c in range(chunks):
                    total = scatter(c, total)
            else:
                total = lax.fori_loop(0, chunks, scatter, total)
            total = total.reshape(row_block, pband, lon)
            for r in range(row_block):
                for b in range(pband // 8):
                    sub = slice(b * 8, (b + 1) * 8)
                    cells[p, first + r, sub, :] = (
                        cells[p, first + r, sub, :] + total[r, sub, :]
                    ) * inv_b[first + r]

    def one_part(p, c):
        pltpu.make_async_copy(
            cells.at[p, pl.ds(0, n - 1)], cells.at[p, pl.ds(0, n - 1)], go_recv.at[p]
        ).wait()
        transport(p)
        nest(p)

        def send_back(t, r):
            pltpu.make_async_remote_copy(
                src_ref=cells.at[p, t * spec + r],
                dst_ref=inbox.at[p, me],
                send_sem=back_send.at[p],
                recv_sem=back_recv.at[p],
                device_id={"space": t, "spec": r},
                device_id_type=MESH,
            ).start()

        peers(send_back)
        inbox[p, me] = cells[p, me]
        return c

    lax.fori_loop(0, parts, one_part, 0)

    for p in range(parts):
        arrived = inbox.at[p, pl.ds(0, n - 1)]
        pltpu.make_async_copy(arrived, arrived, back_recv.at[p]).wait()
        rows_p = slice(p * width_p, (p + 1) * width_p)
        if band % 8 == 0:
            field[rows_p, :] = inbox[p].reshape(width_p, lon)
        else:
            for q in range(n):
                field[q * band : (q + 1) * band, :] = inbox[0, q, 0:band, :]
        turned = field[rows_p, :].T.astype(BF16)
        one = jnp.dot(turned, w1[rows_p, :], preferred_element_type=F32)
        two = jnp.dot(turned, w2[rows_p, :], preferred_element_type=F32)
        if p > 0:
            one = one + sums[0]
            two = two + sums[1]
        if p < parts - 1:
            sums[0] = one
            sums[1] = two
    product = (one * two).astype(BF16)
    for p in range(parts):
        rows_p = slice(p * width_p, (p + 1) * width_p)
        out[rows_p, :] = (field[rows_p, :] + third(product, p)) * own_mask

    pltpu.make_async_copy(
        meta.at[pl.ds(0, tiles - 1)], meta.at[pl.ds(0, tiles - 1)], meta_send
    ).wait()
    for p in range(parts):
        sent = outbox.at[p, pl.ds(0, n - 1)]
        pltpu.make_async_copy(sent, sent, go_send.at[p]).wait()
        sent = cells.at[p, pl.ds(0, n - 1)]
        pltpu.make_async_copy(sent, sent, back_send.at[p]).wait()


def shards(
    spectra,
    quad_first,
    quad_second,
    quad_output,
    owner_map,
    land_mask,
    nest_dest,
    nest_src,
    nest_into,
):
    spec = lax.axis_size("spec")
    tiles = lax.axis_size("space")
    n = spec * tiles
    bins, _, lon = spectra.shape
    band = bins // n
    parts = PARTS if band % (8 * PARTS) == 0 else 1
    pband = band // parts if band % 8 == 0 else -(-band // 8) * 8
    entries = nest_dest.shape[0]
    width = min(entries, lon)
    erows = entries // width
    meta_rows = -(-(-(-spec // 8) * 8 + 3 * erows) // 8) * 8
    total = tiles * entries
    chunk = max(entries, min(2 * lon, total))
    chunks = total // chunk
    dims = (n, tiles, spec, bins, lon, band, parts, pband, entries)
    vmem = pl.BlockSpec(memory_space=pltpu.VMEM)
    hbm = pl.BlockSpec(memory_space=pltpu.HBM)
    V = pltpu.VMEM
    dma = pltpu.SemaphoreType.DMA
    result = pl.pallas_call(
        functools.partial(kernel, dims),
        out_shape=jax.ShapeDtypeStruct((bins, lon), F32),
        in_specs=[hbm] * 9,
        out_specs=vmem,
        scratch_shapes=[
            pltpu.SMEM(owner_map.shape, jnp.int32),
            V(land_mask.shape, jnp.int32),
            V((erows, width), jnp.int32),
            V((erows, width), jnp.int32),
            V((erows, width), jnp.int32),
            V((bins, lon), F32),
            V(quad_first.shape, BF16),
            V(quad_second.shape, BF16),
            V(quad_output.shape, BF16),
            V((parts, n, pband, lon), F32),
            V((parts, n, pband, lon), F32),
            V((parts, n, pband, lon), F32),
            V((2, lon, bins), F32),
            V((tiles, meta_rows, lon), jnp.int32),
            V((4, total // lon, 8, lon), jnp.int32),
            V((n, 8, lon), F32),
            V((n, 8, lon), F32),
            V((4, tiles, parts, pband, lon), F32),
            V((2, parts, pband, lon), F32),
            V((chunks, 2 * lon, chunk), BF16),
            V((chunks, lon, 2 * chunk), BF16),
            V((chunks, pband, chunk), F32),
            dma((9,)),
            dma,
            dma,
            dma((parts,)),
            dma((parts,)),
            dma((parts,)),
            dma((parts,)),
        ],
        compiler_params=pltpu.CompilerParams(
            collective_id=0, has_side_effects=True, vmem_limit_bytes=56 * 1024 * 1024
        ),
        cost_estimate=pl.CostEstimate(
            flops=12 * bins * bins * lon, bytes_accessed=6 * bins * bins + 8 * bins * lon, transcendentals=0
        ),
    )(
        spectra.reshape(bins, lon),
        quad_first,
        quad_second,
        quad_output,
        owner_map,
        land_mask,
        nest_dest.reshape(erows, width),
        nest_src.reshape(erows, width),
        nest_into.reshape(erows, width),
    )
    return result.reshape(spectra.shape)


def solution(mesh):
    return jax.shard_map(
        shards,
        mesh=mesh,
        in_specs=(
            P(None, ("space", "spec"), None),
            P(),
            P(),
            P(),
            P(),
            P("space", None),
            P("space"),
            P("space"),
            P("space"),
        ),
        out_specs=P(None, ("space", "spec"), None),
        check_vma=False,
    )
```
